256 devices in a mesh: dp: 32 (over x, y, core), tp: 8 (over z).
Axes of the slice: x: 4, y: 4, z: 8, core: 2. Of those that a mesh axis runs over, the one named last changes fastest.
Arguments:
- hidden_in: bfloat16 [8192, 7168], P('dp', 'tp'), may hold values from -6 to 6
- kv_down: bfloat16 [7168, 576], P('tp'), may hold values from -0.0625 to 0.0625
- latent_gain: float32 [512], replicated, may hold values from 0.5 to 1.5
- q_nope: bfloat16 [8192, 16384], P('dp', 'tp'), may hold values from -6 to 6
- q_rope: bfloat16 [8192, 8192], P('dp', 'tp'), may hold values from -24 to 24
- absorb_k: bfloat16 [128, 128, 512], P('tp'), may hold values from -0.5 to 0.5
- absorb_v: bfloat16 [128, 512, 128], P('tp'), may hold values from -1 to 1
- store: bfloat16 [1536, 64, 576], P('dp'), may hold values from -25 to 25
- page_owner: int32 [64, 16, 1], P('dp'), may hold values from 0 to 31; in each aligned block of 32 rows (0 to 31, 32 to 63, ..., all dimensions but the last counted through in order) at most 2 rows name the same one
- page_slot: int32 [64, 16], P('dp'), may hold values from 0 to 47
- prefix_len: int32 [64], P('dp'), may hold values from 256 to 1024, as said below
Outputs:
- attn_out: bfloat16 [8192, 16384], P('dp', 'tp')
- new_latent: bfloat16 [8192, 576], P('dp')
The draws below stay inside these ranges and needn't reach their ends.
Inputs may be any that keep to these rules, and one draw needn't show every extreme that they name: `page_owner`: in each aligned block of 32 entries (the requests of one index of dp) no owner is named more than 2 times, and in some block one owner is named exactly 2 times. `prefix_len`: one request at least has a cached prefix of exactly 1024 tokens.
All inputs are finite; a program needn't handle non-finite values.
Results may differ from the reference program's by a relative error of at most 0.0068.
Values may be sent and summed in bfloat16 or wider, within the bound.
No kernel may reach another device: no remote copies, remote signals or barrier semaphores. Data moves between devices by JAX's collectives and lax.ppermute only.
A program may use at most 128 MiB of HBM per device.

```python
import math
import jax
import jax.numpy as jnp
import numpy as np
from jax import lax

D = 7168
HEADS = 128
NOPE = 128
ROPE = 64
KV_RANK = 512
VDIM = 128
PAGE = 64
PMAX = 16
NEW = 128
R_DEV = 2
PAGES_DEV = 48
LAT = 576
CAP = 2
TOKENS = 8192
REQS = 64
PAGES = 1536
N_DP = 32


def draw_q_rope(key, part):
    key = jax.random.fold_in(key, 11)
    key_base = jax.random.fold_in(key, 0)
    values = jnp.clip(jax.random.normal(key_base, (TOKENS, HEADS * ROPE), jnp.float32), -4.0, 4.0)
    return values.astype(jnp.bfloat16)


def draw_store(key, part):
    key = jax.random.fold_in(key, 12)
    values = jnp.clip(jax.random.normal(key, (PAGES, PAGE, LAT), jnp.float32), -6.0, 6.0)
    return values.astype(jnp.bfloat16)


def draw_prefix_len(key, part):
    key = jax.random.fold_in(key, 13)
    key_len, key_longest = jax.random.split(key)
    lengths = jax.random.randint(key_len, (REQS,), PMAX * PAGE // 4, PMAX * PAGE + 1)
    longest = jax.random.randint(key_longest, (), 0, REQS)
    return jnp.where(jnp.arange(REQS) == longest, PMAX * PAGE, lengths).astype(jnp.int32)


def set_ends(entries, stream_key, smallest, high):
    longest = entries.shape.index(max(entries.shape))
    spots = []
    for shift in (0, 1):
        where = [jax.random.randint(jax.random.fold_in(stream_key, axis), (), 0, length) for axis, length in enumerate(entries.shape)]
        where[longest] = (where[longest] + shift) % entries.shape[longest]
        spots.append(tuple(where))
    return entries.at[spots[0]].set(smallest).at[spots[1]].set(high)


def levels(own_key, shape, cuts, least, top_value):
    gain, own = 1.0, jax.random.fold_in(own_key, 6)
    for dim, blocks in cuts:
        heights = jnp.exp(jax.random.uniform(jax.random.fold_in(own, dim), (blocks,), jnp.float32, least / len(cuts), top_value / len(cuts)))
        gain = gain * jnp.repeat(heights, shape[dim] // blocks).reshape([-1 if axis == dim else 1 for axis in range(len(shape))])
    return gain


def routed_block(key, own, number, rows, count, top, limit, lean):
    sequence = jax.random.permutation(key, count)
    packed, ordinary = portions_of(count, rows * top, limit, lean, True), portions_of(count, rows * top, limit, lean, False)
    places = jnp.arange(count)

    def named(sizes, offset_by):
        used = int((sizes > 0).sum())
        fixed = max(1, used // 4)
        moved = fixed + (places - fixed + offset_by * (used - fixed)) % max(1, count - fixed)
        return jnp.zeros((count,), jnp.int32).at[sequence[jnp.where(places < fixed, places, moved)]].set(jnp.asarray(sizes, jnp.int32))

    sizes = jnp.where(number % 4 == 0, named(packed, number // 4), named(ordinary, number - number // 4 - 1))
    mixed = jax.random.permutation(jax.random.fold_in(own, 3), count)
    donor, taker = mixed[0:count // 2 * 2:2], mixed[1:count // 2 * 2:2]
    room = jnp.minimum(sizes[donor] - 1, limit - sizes[taker]) // 2
    room = jnp.where((donor == sequence[0]) | (taker == sequence[0]) | (sizes[taker] == 0), 0, jnp.maximum(room, 0))
    moved = jax.random.randint(jax.random.fold_in(own, 4), (count // 2,), 0, 1 << 20) % (room + 1)
    sizes = sizes.at[donor].add(-moved).at[taker].add(moved)
    members = jnp.searchsorted(jnp.cumsum(sizes), jnp.arange(rows * top), side="right").astype(jnp.int32)
    grid = members.reshape(top, rows).T
    grid = grid[jax.random.permutation(jax.random.fold_in(own, 1), rows)]
    offset_by = jax.random.randint(jax.random.fold_in(own, 2), (rows, 1), 0, top)
    return jnp.take_along_axis(grid, (jnp.arange(top)[None, :] + offset_by) % top, axis=1)


def portions_of(number_of, total, limit, lean, full):
    weights = [(1 << 20) // math.isqrt(standing ** lean) + 1 for standing in range(1, number_of + 1)]
    largest = limit if full else min(limit, max(-(-total // number_of), total * weights[0] // sum(weights)))
    least = 1 if total - largest >= number_of - 1 else 0
    holding, surplus = [largest] + [least] * (number_of - 1), total - largest - least * (number_of - 1)
    while surplus > 0:
        free = [i for i in range(1, number_of) if holding[i] < largest] or [i for i in range(1, number_of) if holding[i] < limit]
        mass, budget = sum([weights[i] for i in free]), surplus
        for i in free:
            extra = min(limit - holding[i], max(1, budget * weights[i] // mass), surplus)
            holding[i] = holding[i] + extra
            surplus = surplus - extra
    return np.array(holding)


def bell_draw(stream_key, shape, scale, most, cuts=(), kind=jnp.bfloat16):
    drawn = jax.random.normal(stream_key, shape, jnp.float32) * scale
    if len(cuts) > 0:
        drawn = levels(stream_key, shape, cuts, -0.22, 0.18) * drawn
    return jnp.clip(drawn, min=-most, max=most).astype(kind)


def setup_inputs(seed: int = 0) -> dict:
    splits = jax.random.split(jax.random.key(seed), 12)
    hidden_in = bell_draw(splits[0], (TOKENS, D), 1.0, 6.0, ((0, 32), (1, 8)))
    kv_down = bell_draw(splits[1], (D, LAT), D ** -0.5, 0.0625, ((0, 8),))
    latent_gain = jnp.clip(1.0 + 0.1 * jax.random.normal(splits[2], (KV_RANK,), jnp.float32), 0.5, 1.5)
    q_nope = bell_draw(splits[3], (TOKENS, HEADS * NOPE), 1.0, 6.0, ((0, 32), (1, 8)))
    q_rope = draw_q_rope(jax.random.fold_in(splits[11], 71), 0)
    absorb_k = bell_draw(splits[5], (HEADS, NOPE, KV_RANK), NOPE ** -0.5, 0.5, ((0, 8),))
    absorb_v = bell_draw(splits[6], (HEADS, KV_RANK, VDIM), (KV_RANK // 16) ** -0.5, 1.0, ((0, 8),))
    store = draw_store(jax.random.fold_in(splits[11], 71), 0)
    page_owner_keys = jax.random.split(jax.random.fold_in(splits[8], 1), REQS * PMAX // (R_DEV * PMAX))
    page_owner_turns = jax.random.permutation(jax.random.fold_in(splits[8], 3), REQS * PMAX // (R_DEV * PMAX))
    page_owner = jax.vmap(lambda own, number: routed_block(jax.random.fold_in(splits[8], 2), own, number, R_DEV * PMAX, N_DP, 1, CAP, 2))(page_owner_keys, page_owner_turns).reshape((REQS, PMAX, 1))
    page_slot = set_ends(jax.random.randint(splits[9], (REQS, PMAX), 0, PAGES_DEV), jax.random.fold_in(splits[9], 1), 0, PAGES_DEV - 1).astype(jnp.int32)
    prefix_len = draw_prefix_len(jax.random.fold_in(splits[11], 71), 0)
    return {"hidden_in": hidden_in, "kv_down": kv_down, "latent_gain": latent_gain, "q_nope": q_nope, "q_rope": q_rope, "absorb_k": absorb_k, "absorb_v": absorb_v, "store": store, "page_owner": page_owner, "page_slot": page_slot, "prefix_len": prefix_len}


def rope_rotate(rotated, position):
    half_width = rotated.shape[-1] // 2
    frequency = 10000.0 ** (-jnp.arange(half_width, dtype=jnp.float32) / half_width)
    angles = position[:, None].astype(jnp.float32) * frequency[None, :]
    cosine = jnp.cos(angles)
    sine_part = jnp.sin(angles)
    first_half = rotated[:, :half_width]
    second_half = rotated[:, half_width:]
    return jnp.concatenate([first_half * cosine - second_half * sine_part, second_half * cosine + first_half * sine_part], axis=1)

def finish_latent(raw_latent, latent_gain, position):
    width = latent_gain.shape[0]
    compressed = raw_latent[:, :width]
    mean_square = lax.optimization_barrier(jnp.mean(compressed * compressed, axis=1, keepdims=True))
    normed = compressed * lax.rsqrt(mean_square + 1e-06) * latent_gain[None, :]
    turned = rope_rotate(raw_latent[:, width:], position)
    return jnp.concatenate([normed, turned], axis=1).astype(jnp.bfloat16)

def reference(hidden_in, kv_down, latent_gain, q_nope, q_rope, absorb_k, absorb_v, store, page_owner, page_slot, prefix_len):
    raw_latent = jnp.dot(hidden_in, kv_down, preferred_element_type=jnp.float32)
    token_ids = jnp.arange(TOKENS, dtype=jnp.int32)
    position = prefix_len[token_ids // NEW] + token_ids % NEW
    new_latent = finish_latent(raw_latent, latent_gain, position)
    page_ids = (page_owner[:, :, 0] * PAGES_DEV + page_slot).astype(jnp.int32)
    scale = 1.0 / jnp.sqrt(jnp.float32(NOPE + ROPE))
    cached_cap = PMAX * PAGE

    def per_request(inputs):
        query_nope, query_rope, new_keys, request_pages, cached_len = inputs
        q_latent = jnp.einsum('thn,hnc->thc', query_nope.astype(jnp.float32), absorb_k.astype(jnp.float32)).astype(jnp.bfloat16)
        q_full = jnp.concatenate([q_latent, query_rope], axis=2)
        cached_keys = store[request_pages].reshape(cached_cap, LAT)
        keys = jnp.concatenate([cached_keys, new_keys], axis=0)
        scores = jnp.einsum('thc,kc->htk', q_full.astype(jnp.float32), keys.astype(jnp.float32)) * scale
        key_idx = jnp.arange(cached_cap + NEW, dtype=jnp.int32)[None, :]
        tok_idx = jnp.arange(NEW, dtype=jnp.int32)[:, None]
        usable = jnp.where(key_idx < cached_cap, key_idx < cached_len, key_idx - cached_cap <= tok_idx)
        scores = jnp.where(usable[None], scores, -1e+30)
        row_max = lax.optimization_barrier(jnp.max(scores, axis=2, keepdims=True))
        expo = jnp.exp(scores - row_max)
        total = lax.optimization_barrier(jnp.sum(expo, axis=2, keepdims=True))
        probs = expo.astype(jnp.bfloat16)
        lat_out = jnp.einsum('htk,kc->thc', probs.astype(jnp.float32), keys[:, :KV_RANK].astype(jnp.float32))
        lat_out = (lat_out / jnp.transpose(total, (1, 0, 2))).astype(jnp.bfloat16)
        result = jnp.einsum('thc,hcv->thv', lat_out.astype(jnp.float32), absorb_v.astype(jnp.float32))
        return result.astype(jnp.bfloat16).reshape(NEW, HEADS * VDIM)
    outputs = lax.map(per_request, (q_nope.reshape(REQS, NEW, HEADS, NOPE), q_rope.reshape(REQS, NEW, HEADS, ROPE), new_latent.reshape(REQS, NEW, LAT), page_ids, prefix_len))
    return (outputs.reshape(TOKENS, HEADS * VDIM), new_latent)
```

```python
import functools
import math

import jax
import jax.numpy as jnp
from jax import lax
from jax.experimental import pallas as pl
from jax.experimental.pallas import tpu as pltpu
from jax.sharding import PartitionSpec as P

BF16 = jnp.bfloat16
F32 = jnp.float32
MASKED = -1e30
LANES = 128


def rope_rotate(rotated, position):
    half_width = rotated.shape[-1] // 2
    frequency = 10000.0 ** (-jnp.arange(half_width, dtype=F32) / half_width)
    angles = position[:, None].astype(F32) * frequency[None, :]
    cosine = jnp.cos(angles)
    sine_part = jnp.sin(angles)
    first_half = rotated[:, :half_width]
    second_half = rotated[:, half_width:]
    return jnp.concatenate(
        [
            first_half * cosine - second_half * sine_part,
            second_half * cosine + first_half * sine_part,
        ],
        axis=1,
    )


def finish_latent(raw_latent, latent_gain, position):
    width = latent_gain.shape[0]
    compressed = raw_latent[:, :width]
    mean_square = jnp.mean(compressed * compressed, axis=1, keepdims=True)
    normed = compressed * lax.rsqrt(mean_square + 1e-06) * latent_gain[None, :]
    turned = rope_rotate(raw_latent[:, width:], position)
    return jnp.concatenate([normed, turned], axis=1).astype(BF16)


def plan_body(owner_ref, slot_ref, want_ref, pick_ref):
    places = want_ref.shape[0]
    entries = pick_ref.shape[0]
    for i in range(places):
        want_ref[i] = -1
    for i in range(entries):
        first = 2 * owner_ref[i]
        place = first + jnp.where(want_ref[first] < 0, 0, 1)
        want_ref[place] = slot_ref[i]
        pick_ref[i] = place


def plan(owners, slots, places):
    smem = pl.BlockSpec(memory_space=pltpu.SMEM)
    return pl.pallas_call(
        plan_body,
        out_shape=(
            jax.ShapeDtypeStruct((places,), jnp.int32),
            jax.ShapeDtypeStruct(owners.shape, jnp.int32),
        ),
        in_specs=[smem, smem],
        out_specs=(smem, smem),
        name="plan",
    )(owners, slots)


def gather_body(ids_ref, pages_ref, out_ref):
    last = pages_ref.shape[0] - 1
    for i in range(out_ref.shape[0]):
        out_ref[i] = pages_ref[jnp.clip(ids_ref[i], 0, last)]


def gather_pages(ids, pages):
    return pl.pallas_call(
        gather_body,
        out_shape=jax.ShapeDtypeStruct((ids.shape[0],) + pages.shape[1:], pages.dtype),
        in_specs=[
            pl.BlockSpec(memory_space=pltpu.SMEM),
            pl.BlockSpec(memory_space=pltpu.VMEM),
        ],
        out_specs=pl.BlockSpec(memory_space=pltpu.VMEM),
        name="gather_pages",
    )(ids, pages)


def select_body(pick_ref, fetched_ref, out_ref, *, cols):
    entries = pick_ref.shape[0]
    per_req = entries // 2
    rows = 2 * fetched_ref.shape[1]
    width = cols * LANES
    for i in range(per_req // 2):
        tails = []
        for r in range(2):
            first = pick_ref[r * per_req + 2 * i]
            second = pick_ref[r * per_req + 2 * i + 1]
            both = jnp.concatenate(
                [fetched_ref[first].astype(F32), fetched_ref[second].astype(F32)], axis=0
            )
            at = r * LANES + i * rows
            for c in range(cols):
                out_ref[pl.ds(c * 2 * LANES + at, rows), :] = both[
                    :, c * LANES : (c + 1) * LANES
                ].astype(BF16)
            tails.append(both[:, width:])
        out_ref[pl.ds(cols * 2 * LANES + i * rows, rows), :] = jnp.concatenate(
            tails, axis=1
        ).astype(BF16)


def select_pages(pick, fetched, cols):
    return pl.pallas_call(
        functools.partial(select_body, cols=cols),
        out_shape=jax.ShapeDtypeStruct(((2 * cols + 1) * LANES, LANES), BF16),
        in_specs=[
            pl.BlockSpec(memory_space=pltpu.SMEM),
            pl.BlockSpec(memory_space=pltpu.VMEM),
        ],
        out_specs=pl.BlockSpec(memory_space=pltpu.VMEM),
        name="select_pages",
    )(pick, fetched)


def query_body(nope_ref, rope_ref, absorb_ref, out_ref):
    rows = nope_ref.shape[0]
    half = rows // 2
    nope = absorb_ref.shape[1]
    width = absorb_ref.shape[2]
    rope = rope_ref[...].astype(F32)
    turned = pltpu.roll(rope, LANES // 2, 1)
    low = lax.broadcasted_iota(jnp.int32, (half, LANES), 1) < LANES // 2
    for h in range(2):
        latent = jnp.dot(
            nope_ref[:, h * nope : (h + 1) * nope], absorb_ref[h], preferred_element_type=F32
        )
        out_ref[h, :, :width] = latent.astype(BF16)
        at_low, at_high = (rope, turned) if h == 0 else (turned, rope)
        out_ref[h, :half, width:] = jnp.where(low, at_low[:half], 0.0).astype(BF16)
        out_ref[h, half:, width:] = jnp.where(low, 0.0, at_high[half:]).astype(BF16)


def queries(q_nope, q_rope, absorb_k):
    rows = q_nope.shape[0]
    heads, nope, width = absorb_k.shape
    full = width + LANES
    return pl.pallas_call(
        query_body,
        grid=(heads // 2,),
        out_shape=jax.ShapeDtypeStruct((heads, rows, full), BF16),
        in_specs=[
            pl.BlockSpec((rows, 2 * nope), lambda i: (0, i)),
            pl.BlockSpec((rows, LANES), lambda i: (0, i)),
            pl.BlockSpec((2, nope, width), lambda i: (i, 0, 0)),
        ],
        out_specs=pl.BlockSpec((2, rows, full), lambda i: (i, 0, 0)),
        cost_estimate=pl.CostEstimate(
            flops=2 * rows * heads * nope * width,
            bytes_accessed=2 * (rows * heads * (nope + full) + heads * nope * width),
            transcendentals=0,
        ),
        name="queries",
    )(q_nope, q_rope, absorb_k)


def attend_body(*refs, pieces, has_new, first, last, factor, page, split):
    refs = list(refs)
    origin_ref = refs.pop(0)
    prefix_ref = refs.pop(0)
    query_ref = refs.pop(0)
    blocks = []
    for count in pieces:
        blocks.append([refs.pop(0) for _ in range(count)])
    if not first:
        acc_in, stat_in = refs.pop(0), refs.pop(0)
    if last:
        absorb_ref = refs.pop(0)
        out_ref = refs.pop(0)
    else:
        acc_out, stat_out = refs.pop(0), refs.pop(0)
    keys_ref, bias_ref = refs
    group, tokens, full = query_ref.shape
    width = full - LANES
    cols = width // LANES
    count = len(pieces)
    r = pl.program_id(0)

    @pl.when(pl.program_id(1) == 0)
    def _():
        for b, parts in enumerate(blocks):
            at = pl.ds(b * LANES, LANES)
            starts = []
            for part in parts:
                starts += [(part, i) for i in range(0, part.shape[0], LANES)]
            for c in range(cols):
                lows = starts[2 * c]
                keys_ref[at, c * LANES : (c + 1) * LANES] = lows[0][
                    pl.ds(lows[1] + r * LANES, LANES), :
                ]
            tail = starts[2 * cols]
            keys_ref[at, width:] = tail[0][pl.ds(tail[1], LANES), :]
            place = lax.broadcasted_iota(jnp.int32, (tokens, LANES), 1)
            if has_new and b == count - 1:
                token = lax.broadcasted_iota(jnp.int32, (tokens, LANES), 0)
                used = place <= token
            else:
                position = place // split * page + origin_ref[b] * split + place % split
                used = position < prefix_ref[r]
            bias_ref[:, b * LANES : (b + 1) * LANES] = jnp.where(used, 0.0, MASKED)

    keys = keys_ref[...]
    bias = bias_ref[...]
    for h in range(0, group, 2):
        q = query_ref[h : h + 2].reshape(2 * tokens, full)
        scores = lax.dot_general(
            q, keys, (((1,), (1,)), ((), ())), preferred_element_type=F32
        )
        scores = scores + jnp.concatenate([bias, bias], axis=0)
        top = jnp.max(scores, axis=1, keepdims=True)
        if not first:
            stat = stat_in[h : h + 2].reshape(2 * tokens, LANES)
            old_top = stat[:, 0:1]
            top = jnp.maximum(top, old_top)
        expo = jnp.exp2((scores - top) * factor)
        total = jnp.sum(expo, axis=1, keepdims=True)
        acc = jnp.dot(expo.astype(BF16), keys[:, :width], preferred_element_type=F32)
        if not first:
            alpha = jnp.exp2((old_top - top) * factor)
            total = total + alpha * stat[:, LANES // 2 : LANES // 2 + 1]
            acc = acc + alpha * acc_in[h : h + 2].reshape(2 * tokens, width).astype(F32)
        if last:
            latent = (acc / total).astype(BF16)
            for k in range(2):
                vdim = absorb_ref.shape[2]
                out_ref[:, (h + k) * vdim : (h + k + 1) * vdim] = jnp.dot(
                    latent[k * tokens : (k + 1) * tokens],
                    absorb_ref[h + k],
                    preferred_element_type=F32,
                ).astype(BF16)
        else:
            low = lax.broadcasted_iota(jnp.int32, (2 * tokens, LANES), 1) < LANES // 2
            acc_out[h : h + 2] = acc.astype(acc_out.dtype).reshape(2, tokens, width)
            stat_out[h : h + 2] = jnp.where(low, top, total).reshape(2, tokens, LANES)


def attend(query, blocks, origins, prefix_len, state, absorb_v, has_new, factor, page, split, group=4):
    heads, rows, full = query.shape
    width = full - LANES
    tokens = rows // 2
    first, last = state is None, absorb_v is not None
    smem = pl.BlockSpec(memory_space=pltpu.SMEM)
    by_head = lambda r, g: (g, r, 0)
    in_specs = [smem, smem, pl.BlockSpec((group, tokens, full), by_head)]
    args = [origins, prefix_len, query]
    for parts in blocks:
        for part in parts:
            in_specs.append(pl.BlockSpec(part.shape, lambda r, g: (0, 0)))
            args.append(part)
    acc_spec = pl.BlockSpec((group, tokens, width), by_head)
    stat_spec = pl.BlockSpec((group, tokens, LANES), by_head)
    if not first:
        in_specs += [acc_spec, stat_spec]
        args += list(state)
    if last:
        vdim = absorb_v.shape[2]
        in_specs.append(pl.BlockSpec((group, width, vdim), lambda r, g: (g, 0, 0)))
        args.append(absorb_v)
        out_shape = jax.ShapeDtypeStruct((rows, heads * vdim), BF16)
        out_specs = pl.BlockSpec((tokens, group * vdim), lambda r, g: (r, g))
    else:
        out_shape = (
            jax.ShapeDtypeStruct((heads, rows, width), BF16),
            jax.ShapeDtypeStruct((heads, rows, LANES), F32),
        )
        out_specs = (acc_spec, stat_spec)
    keys = len(blocks) * LANES
    flops = 2 * heads * rows * keys * (full + width)
    return pl.pallas_call(
        functools.partial(
            attend_body,
            pieces=tuple(len(p) for p in blocks),
            has_new=has_new,
            first=first,
            last=last,
            factor=factor,
            page=page,
            split=split,
        ),
        grid=(2, heads // group),
        out_shape=out_shape,
        in_specs=in_specs,
        out_specs=out_specs,
        scratch_shapes=[pltpu.VMEM((keys, full), BF16), pltpu.VMEM((tokens, keys), F32)],
        compiler_params=pltpu.CompilerParams(vmem_limit_bytes=48 << 20),
        cost_estimate=pl.CostEstimate(
            flops=flops,
            bytes_accessed=2 * heads * rows * (full + 2 * width),
            transcendentals=heads * rows * keys,
        ),
        name="attend",
    )(*args)


def shards(
    hidden_in,
    kv_down,
    latent_gain,
    q_nope,
    q_rope,
    absorb_k,
    absorb_v,
    store,
    page_owner,
    page_slot,
    prefix_len,
):
    rows = hidden_in.shape[0]
    reqs = prefix_len.shape[0]
    new_len = rows // reqs
    kv_rank = latent_gain.shape[0]
    lat_width = kv_down.shape[1]
    nope_width = absorb_k.shape[1]
    rope_width = lat_width - kv_rank
    page = store.shape[1]
    dp_size = lax.axis_size("dp")
    tp_size = lax.axis_size("tp")
    z = lax.axis_index("tp")
    split = page // tp_size
    cols = kv_rank // LANES

    want, pick = plan(page_owner.reshape(-1), page_slot.reshape(-1), 2 * dp_size)
    asked = lax.all_to_all(want.reshape(dp_size, 1, 2), "dp", split_axis=0, concat_axis=0, tiled=True)

    part = jnp.dot(hidden_in, kv_down, preferred_element_type=F32)
    step = tp_size // 2
    while step:
        half = part.shape[0] // 2
        upper = (z // step) % 2 == 1
        keep = jnp.where(upper, part[half:], part[:half])
        give = jnp.where(upper, part[:half], part[half:]).astype(BF16)
        got = lax.ppermute(give, "tp", [(i, i ^ step) for i in range(tp_size)])
        part = keep + got.astype(F32)
        step //= 2
    own_rows = rows // tp_size
    token = z * own_rows + jnp.arange(own_rows, dtype=jnp.int32)
    position = jnp.where(token // new_len == 0, prefix_len[0], prefix_len[1]) + token % new_len
    own_latent = finish_latent(part, latent_gain, position)
    new_latent = lax.all_gather(own_latent, "tp", axis=0, tiled=True)
    new_block = jnp.concatenate(
        [new_latent[:, c * LANES : (c + 1) * LANES] for c in range(cols)]
        + [
            jnp.concatenate(
                [new_latent[:new_len, kv_rank:], new_latent[new_len:, kv_rank:]], axis=1
            )
        ],
        axis=0,
    )

    query = queries(q_nope, q_rope, absorb_k)

    piece = lax.dynamic_slice_in_dim(store, z * split, split, axis=1)
    reply = gather_pages(asked.reshape(-1), piece)
    fetched = lax.all_to_all(
        reply.reshape(dp_size, 2, split, lat_width), "dp", split_axis=0, concat_axis=0, tiled=True
    )
    own = select_pages(pick, fetched.reshape(2 * dp_size, split, lat_width), cols)
    up = [(i, (i + 1) % tp_size) for i in range(tp_size)]
    down = [(i, (i - 1) % tp_size) for i in range(tp_size)]
    right, left = [own], [own]
    for _ in range(tp_size // 2 - 1):
        right.append(lax.ppermute(right[-1], "tp", up))
        left.append(lax.ppermute(left[-1], "tp", down))
    cut = cols * LANES
    far = [
        lax.ppermute(right[-1][:cut], "tp", up),
        lax.ppermute(left[-1][cut:], "tp", down),
    ]

    factor = math.log2(math.e) / math.sqrt(nope_width + rope_width)

    def origins(*steps):
        return jnp.stack([(z + s) % tp_size for s in steps]).astype(jnp.int32)

    common = dict(factor=factor, page=page, split=split)
    state = attend(
        query,
        [[right[1]], [left[1]], [own]],
        origins(-1, 1, 0),
        prefix_len,
        None,
        None,
        False,
        **common,
    )
    state = attend(
        query,
        [[right[2]], [left[2]], [right[3]], [left[3]]],
        origins(-2, 2, -3, 3),
        prefix_len,
        state,
        None,
        False,
        **common,
    )
    attn_out = attend(
        query,
        [far, [new_block]],
        origins(4, 0),
        prefix_len,
        state,
        absorb_v,
        True,
        **common,
    )
    return attn_out, new_latent


def solution(mesh):
    placed = (
        P("dp", "tp"),
        P("tp", None),
        P(),
        P("dp", "tp"),
        P("dp", "tp"),
        P("tp", None, None),
        P("tp", None, None),
        P("dp", None, None),
        P("dp", None, None),
        P("dp", None),
        P("dp"),
    )
    return jax.shard_map(
        shards,
        mesh=mesh,
        in_specs=placed,
        out_specs=(P("dp", "tp"), P("dp", None)),
        check_vma=False,
    )
```

```python
import functools
import math

import jax
import jax.numpy as jnp
from jax import lax
from jax.experimental import pallas as pl
from jax.experimental.pallas import tpu as pltpu
from jax.sharding import PartitionSpec as P

BF16 = jnp.bfloat16
F32 = jnp.float32
MASKED = -1e30
LANES = 128


def turn_tables(position, half_width):
    frequency = 10000.0 ** (-jnp.arange(half_width, dtype=F32) / half_width)
    angles = position[:, None].astype(F32) * frequency[None, :]
    return jnp.cos(angles), jnp.sin(angles)


VMEM = pl.BlockSpec(memory_space=pltpu.VMEM)
SMEM = pl.BlockSpec(memory_space=pltpu.SMEM)
SMALL = pltpu.CompilerParams(vmem_limit_bytes=4 << 20)


def deal_body(place_ref, hidden_ref, down_ref, keep_ref, *rest):
    part_ref = rest[-1]
    part_ref[...] = lax.dot_general(
        hidden_ref[...], down_ref[...], (((1,), (1,)), ((), ())), preferred_element_type=F32
    )
    rows = keep_ref.shape[0]
    keep_ref[...] = part_ref[pl.ds(pl.multiple_of(place_ref[0] * rows, rows), rows), :]
    for i, give_ref in enumerate(rest[:-1]):
        other = pl.multiple_of(place_ref[1 + i] * rows, rows)
        give_ref[...] = part_ref[pl.ds(other, rows), :].astype(BF16)


def deal(place, hidden, down, members):
    rows, width = hidden.shape[0] // members, down.shape[0]
    return pl.pallas_call(
        deal_body,
        out_shape=(jax.ShapeDtypeStruct((rows, width), F32),)
        + (jax.ShapeDtypeStruct((rows, width), BF16),) * (members - 1),
        in_specs=[SMEM, VMEM, VMEM],
        out_specs=(VMEM,) * members,
        scratch_shapes=[pltpu.VMEM((hidden.shape[0], width), F32)],
        compiler_params=SMALL,
        name="deal",
    )(place, hidden, down)


def finish_body(kept_ref, gain_ref, cos_ref, sin_ref, *rest):
    out_ref = rest[-1]
    width = gain_ref.shape[1]
    raw = kept_ref[...]
    for got_ref in rest[:-1]:
        raw = raw + got_ref[...].astype(F32)
    compressed = raw[:, :width]
    mean_square = jnp.mean(compressed * compressed, axis=1, keepdims=True)
    latent = (compressed * lax.rsqrt(mean_square + 1e-06) * gain_ref[...]).astype(BF16)
    half = cos_ref.shape[1]
    first, second = raw[:, width : width + half], raw[:, width + half :]
    cosine, sine = cos_ref[...], sin_ref[...]
    turned = jnp.concatenate(
        [first * cosine - second * sine, second * cosine + first * sine], axis=1
    )
    rows = raw.shape[0]
    for c in range(width // LANES):
        out_ref[c * rows : (c + 1) * rows, :] = latent[:, c * LANES : (c + 1) * LANES]
    out_ref[width // LANES * rows :, :] = jnp.concatenate(
        [turned[: rows // 2], turned[rows // 2 :]], axis=1
    ).astype(BF16)


def finish_latents(kept, gain, cosine, sine, got):
    rows, width = kept.shape[0], gain.shape[1]
    return pl.pallas_call(
        finish_body,
        out_shape=jax.ShapeDtypeStruct((width // LANES * rows + rows // 2, LANES), BF16),
        in_specs=[VMEM] * (4 + len(got)),
        out_specs=VMEM,
        compiler_params=SMALL,
        name="finish_latents",
    )(kept, gain, cosine, sine, *got)


def plan_body(owner_ref, slot_ref, want_ref, pick_ref):
    reqs, pages = owner_ref.shape
    for owner in range(want_ref.shape[0]):
        want_ref[owner, 0, 0] = -1
        want_ref[owner, 0, 1] = -1
    for r in range(reqs):
        for i in range(pages):
            owner = owner_ref[r, i]
            rank = jnp.where(want_ref[owner, 0, 0] < 0, 0, 1)
            want_ref[owner, 0, rank] = slot_ref[r, i]
            pick_ref[r * pages + i] = 2 * owner + rank


def plan(owners, slots, dp_size):
    smem = pl.BlockSpec(memory_space=pltpu.SMEM)
    return pl.pallas_call(
        plan_body,
        out_shape=(
            jax.ShapeDtypeStruct((dp_size, 1, 2), jnp.int32),
            jax.ShapeDtypeStruct((owners.size,), jnp.int32),
        ),
        in_specs=[smem, smem],
        out_specs=(smem, smem),
        name="plan",
    )(owners, slots)


def gather_body(ids_ref, pages_ref, out_ref):
    last = pages_ref.shape[0] - 1
    for i in range(ids_ref.shape[0]):
        for j in range(2):
            out_ref[i, j] = pages_ref[jnp.clip(ids_ref[i, 0, j], 0, last)]


def gather_pages(ids, pages):
    return pl.pallas_call(
        gather_body,
        out_shape=jax.ShapeDtypeStruct((ids.shape[0], 2) + pages.shape[1:], pages.dtype),
        in_specs=[
            pl.BlockSpec(memory_space=pltpu.SMEM),
            pl.BlockSpec(memory_space=pltpu.VMEM),
        ],
        out_specs=pl.BlockSpec(memory_space=pltpu.VMEM),
        compiler_params=pltpu.CompilerParams(vmem_limit_bytes=4 << 20),
        name="gather_pages",
    )(ids, pages)


def select_body(pick_ref, fetched_ref, fresh_ref, out_ref, *, cols):
    out_ref[(2 * cols + 1) * LANES :, :] = fresh_ref[...]
    entries = pick_ref.shape[0]
    per_req = entries // 2
    rows = 2 * fetched_ref.shape[1]
    width = cols * LANES
    for i in range(per_req // 2):
        tails = []
        for r in range(2):
            first = pick_ref[r * per_req + 2 * i]
            second = pick_ref[r * per_req + 2 * i + 1]
            both = jnp.concatenate(
                [fetched_ref[first].astype(F32), fetched_ref[second].astype(F32)], axis=0
            )
            at = r * LANES + i * rows
            for c in range(cols):
                out_ref[pl.ds(c * 2 * LANES + at, rows), :] = both[
                    :, c * LANES : (c + 1) * LANES
                ].astype(BF16)
            tails.append(both[:, width:])
        out_ref[pl.ds(cols * 2 * LANES + i * rows, rows), :] = jnp.concatenate(
            tails, axis=1
        ).astype(BF16)


def select_pages(pick, fetched, fresh, cols):
    return pl.pallas_call(
        functools.partial(select_body, cols=cols),
        out_shape=jax.ShapeDtypeStruct(((2 * cols + 1) * LANES + fresh.shape[0], LANES), BF16),
        in_specs=[
            SMEM,
            VMEM,
            VMEM,
        ],
        out_specs=VMEM,
        compiler_params=SMALL,
        name="select_pages",
    )(pick, fetched, fresh)


def query_body(nope_ref, rope_ref, absorb_ref, out_ref):
    rows = nope_ref.shape[0]
    half = rows // 2
    heads, nope, width = absorb_ref.shape
    side = LANES // 2
    for p in range(heads // 2):
        rope = rope_ref[:, p * LANES : (p + 1) * LANES].T
        for h in range(2):
            n = 2 * p + h
            latent = lax.dot_general(
                absorb_ref[n],
                nope_ref[:, n * nope : (n + 1) * nope],
                (((0,), (1,)), ((), ())),
                preferred_element_type=F32,
            ).astype(BF16)
            at = slice(h * LANES, (h + 1) * LANES)
            for r in range(2):
                out_ref[p, r, :width, at] = latent[:, r * half : (r + 1) * half]
                put, skip = width + r * side, width + (1 - r) * side
                out_ref[p, r, put : put + side, at] = rope[
                    h * side : (h + 1) * side, r * half : (r + 1) * half
                ]
                out_ref[p, r, skip : skip + side, at] = jnp.zeros((side, LANES), BF16)


def queries(q_nope, q_rope, absorb_k):
    rows = q_nope.shape[0]
    heads, _, width = absorb_k.shape
    vmem = pl.BlockSpec(memory_space=pltpu.VMEM)
    return pl.pallas_call(
        query_body,
        out_shape=jax.ShapeDtypeStruct((heads // 2, 2, width + LANES, rows), BF16),
        in_specs=[vmem] * 3,
        out_specs=vmem,
        compiler_params=pltpu.CompilerParams(vmem_limit_bytes=16 << 20),
        name="queries",
    )(q_nope, q_rope, absorb_k)


def lay_block(parts, b, r, step, origin_ref, prefix_ref, keys_ref, values_ref, bias_ref, page, split):
    width = values_ref.shape[0]
    at = slice(b * LANES, (b + 1) * LANES)
    starts = []
    for part in parts:
        starts += [(part, i) for i in range(0, part.shape[0], LANES)]
    for c in range(width // LANES):
        ref, low = starts[2 * c + r]
        tile = ref[low : low + LANES, :]
        keys_ref[at, c * LANES : (c + 1) * LANES] = tile
        values_ref[c * LANES : (c + 1) * LANES, at] = tile.T
    ref, low = starts[2 * (width // LANES)]
    keys_ref[at, width:] = ref[low : low + LANES, :]
    place = lax.broadcasted_iota(jnp.int32, (LANES, LANES), 0)
    position = place // split * page + origin_ref[step] * split + place % split
    bias_ref[at, :] = jnp.where(position < prefix_ref[r], 0.0, MASKED)


def join_new(tails, origin_ref, new_ref):
    for ref, low, step in tails:
        rows = (ref.shape[0] - low) * 2 // 9
        first = pl.multiple_of(origin_ref[step] * rows, rows)
        for c in range(4):
            new_ref[pl.ds(first, rows), c * LANES : (c + 1) * LANES] = ref[
                low + c * rows : low + (c + 1) * rows, :
            ]
        turned = ref[low + 4 * rows :, :]
        half = rows // 2
        for h in range(2):
            place = pl.multiple_of(first + h * half, half)
            new_ref[pl.ds(place, half), 4 * LANES :] = turned[
                :, h * LANES // 2 : (h + 1) * LANES // 2
            ]


def lay_new(new_ref, b, r, keys_ref, values_ref, bias_ref):
    width = values_ref.shape[0]
    side = LANES // 2
    at = slice(b * LANES, (b + 1) * LANES)
    rows = slice(r * LANES, (r + 1) * LANES)
    for c in range(width // LANES):
        tile = new_ref[rows, c * LANES : (c + 1) * LANES]
        keys_ref[at, c * LANES : (c + 1) * LANES] = tile
        values_ref[c * LANES : (c + 1) * LANES, at] = tile.T
    put, skip = width + r * side, width + (1 - r) * side
    keys_ref[at, put : put + side] = new_ref[rows, width:]
    keys_ref[at, skip : skip + side] = jnp.zeros((LANES, side), BF16)
    place = lax.broadcasted_iota(jnp.int32, (LANES, LANES), 0)
    token = lax.broadcasted_iota(jnp.int32, (LANES, LANES), 1)
    bias_ref[at, :] = jnp.where(place <= token, 0.0, MASKED)


def attend_body(*refs, pieces, steps, seen_steps, full_width, first, last, factor, page, split):
    refs = list(refs)
    origin_ref, prefix_ref, query_ref = [refs.pop(0) for _ in range(3)]
    blocks = [[refs.pop(0) for _ in range(n)] for n in pieces]
    if not first:
        acc_in, stat_in = refs.pop(0), refs.pop(0)
    if last:
        seen = [refs.pop(0) for _ in seen_steps]
        absorb_ref, out_ref, turned_ref, new_ref = [refs.pop(0) for _ in range(3)] + [refs.pop()]
        low = (full_width // LANES * 2 - 1) * LANES
        tails = [(ref, low, step) for ref, step in zip(seen, seen_steps)]
        cut = blocks[0][0].shape[0]
        join_new(tails + [(blocks[0][1], low - cut, steps[0])], origin_ref, new_ref)
    else:
        acc_out, stat_out = refs.pop(0), refs.pop(0)
    keys_ref, values_ref, bias_ref = refs
    pairs, reqs, full, lanes = query_ref.shape

    def score(r, k):
        s = jnp.dot(keys_ref[r], query_ref[k, r], preferred_element_type=F32)
        bias = bias_ref[r]
        return s + jnp.concatenate([bias, bias], axis=1)

    def finish(r, k, s):
        top = jnp.max(s, axis=0, keepdims=True)
        if not first:
            old_top = stat_in[k, r, 0:1, :]
            top = jnp.maximum(top, old_top)
        expo = jnp.exp2((s - top) * factor)
        total = jnp.sum(expo, axis=0, keepdims=True)
        acc = jnp.dot(values_ref[r], expo.astype(BF16), preferred_element_type=F32)
        if not first:
            alpha = jnp.exp2((old_top - top) * factor)
            total = total + alpha * stat_in[k, r, 1:2, :]
            acc = acc + alpha * acc_in[k, r].astype(F32)
        if last:
            latent = (acc * (1.0 / total)).astype(BF16)
            vdim = absorb_ref.shape[2]
            tokens = lanes // 2
            for h in range(2):
                n = 2 * k + h
                out_ref[r * tokens : (r + 1) * tokens, n * vdim : (n + 1) * vdim] = lax.dot_general(
                    latent[:, h * tokens : (h + 1) * tokens],
                    absorb_ref[n],
                    (((0,), (0,)), ((), ())),
                    preferred_element_type=F32,
                ).astype(BF16)
        else:
            acc_out[k, r] = acc.astype(BF16)
            stat_out[k, r, 0:1, :] = top
            stat_out[k, r, 1:2, :] = total

    for r in range(reqs):
        for b, parts in enumerate(blocks):
            lay_block(
                parts, b, r, steps[b], origin_ref, prefix_ref,
                keys_ref.at[r], values_ref.at[r], bias_ref.at[r], page, split,
            )
        if last:
            lay_new(new_ref, len(blocks), r, keys_ref.at[r], values_ref.at[r], bias_ref.at[r])
            own = slice(r * LANES, (r + 1) * LANES)
            turned_ref[: full - LANES, own] = values_ref[r, :, len(blocks) * LANES :]
            turned_ref[full - LANES :, own] = new_ref[own, full - LANES :].T
    order = [(r, k) for r in range(reqs) for k in range(pairs)]
    s = score(*order[0])
    for i, (r, k) in enumerate(order):
        following = score(*order[i + 1]) if i + 1 < len(order) else None
        finish(r, k, s)
        s = following


def attend(
    query, blocks, steps, origins, prefix_len, factor, page, split, state=None, absorb_v=None, seen=()
):
    pairs, reqs, full, lanes = query.shape
    width = full - LANES
    first, last = state is None, absorb_v is not None
    args = [query] + [part for parts in blocks for part in parts]
    aliases = {}
    if not first:
        if not last:
            aliases = {2 + len(args): 0, 3 + len(args): 1}
        args += list(state)
    if last:
        args += [block for _, block in seen] + [absorb_v]
        vdim = absorb_v.shape[2]
        out_shape = (
            jax.ShapeDtypeStruct((reqs * lanes // 2, 2 * pairs * vdim), BF16),
            jax.ShapeDtypeStruct((width + LANES // 2, reqs * lanes // 2), BF16),
        )
    else:
        out_shape = (
            jax.ShapeDtypeStruct((pairs, reqs, width, lanes), BF16),
            jax.ShapeDtypeStruct((pairs, reqs, 8, lanes), F32),
        )
    keys = (len(blocks) + last) * LANES
    return pl.pallas_call(
        functools.partial(
            attend_body,
            pieces=tuple(len(parts) for parts in blocks),
            steps=steps,
            seen_steps=tuple(step for step, _ in seen),
            full_width=full,
            first=first,
            last=last,
            factor=factor,
            page=page,
            split=split,
        ),
        out_shape=out_shape,
        in_specs=[SMEM, SMEM] + [VMEM] * len(args),
        out_specs=(VMEM, VMEM),
        input_output_aliases=aliases,
        scratch_shapes=[
            pltpu.VMEM((reqs, keys, full), BF16),
            pltpu.VMEM((reqs, width, keys), BF16),
            pltpu.VMEM((reqs, keys, LANES), F32),
        ]
        + [pltpu.VMEM((reqs * lanes // 2, width + LANES // 2), BF16)] * last,
        compiler_params=pltpu.CompilerParams(vmem_limit_bytes=16 << 20),
        cost_estimate=pl.CostEstimate(
            flops=2 * pairs * reqs * lanes * keys * (full + width),
            bytes_accessed=2 * pairs * reqs * lanes * (full + 2 * width),
            transcendentals=pairs * reqs * lanes * keys,
        ),
        name="attend",
    )(origins, prefix_len, *args)


def shards(
    hidden_in,
    kv_down,
    latent_gain,
    q_nope,
    q_rope,
    absorb_k,
    absorb_v,
    store,
    page_owner,
    page_slot,
    prefix_len,
):
    rows = hidden_in.shape[0]
    reqs = prefix_len.shape[0]
    new_len = rows // reqs
    kv_rank = latent_gain.shape[0]
    lat_width = kv_down.shape[1]
    nope_width = absorb_k.shape[1]
    rope_width = lat_width - kv_rank
    page = store.shape[1]
    dp_size = lax.axis_size("dp")
    tp_size = lax.axis_size("tp")
    z = lax.axis_index("tp")
    split = page // tp_size
    cols = kv_rank // LANES

    place = jnp.stack([z ^ i for i in range(tp_size)]).astype(jnp.int32)
    origins = ((z + jnp.arange(tp_size, dtype=jnp.int32)) % tp_size).astype(jnp.int32)
    own_rows = rows // tp_size
    token = z * own_rows + jnp.arange(own_rows, dtype=jnp.int32)
    position = jnp.where(token // new_len == 0, prefix_len[0], prefix_len[1]) + token % new_len
    piece = lax.dynamic_slice_in_dim(store, z * split, split, axis=1)

    def swap(given, far):
        return lax.ppermute(given, "tp", [(i, i ^ far) for i in range(tp_size)])

    want, pick = plan(page_owner[:, :, 0], page_slot, dp_size)
    asked = lax.all_to_all(want, "dp", split_axis=0, concat_axis=0, tiled=True)

    reply = gather_pages(asked, piece)
    reply, hidden_in, place, position = lax.optimization_barrier(
        (reply, hidden_in, place, position)
    )
    fetched = lax.all_to_all(reply, "dp", split_axis=0, concat_axis=0, tiled=True)

    cosine, sine = turn_tables(position, rope_width // 2)
    gain = latent_gain[None, :]
    kept, *gives = deal(place, hidden_in, kv_down.T, tp_size)
    got = [swap(given, i + 1) for i, given in enumerate(gives)]
    fresh = finish_latents(kept, gain, cosine, sine, got)
    fetched, fresh, q_nope = lax.optimization_barrier((fetched, fresh, q_nope))

    query = queries(q_nope, q_rope, absorb_k)
    attention = functools.partial(
        attend,
        query,
        origins=origins,
        prefix_len=prefix_len,
        factor=math.log2(math.e) / math.sqrt(nope_width + rope_width),
        page=page,
        split=split,
    )
    up = [(i, (i + 1) % tp_size) for i in range(tp_size)]
    down = [(i, (i - 1) % tp_size) for i in range(tp_size)]
    own = select_pages(pick, fetched.reshape(2 * dp_size, split, lat_width), fresh, cols)
    right, left = lax.ppermute(own, "tp", up), lax.ppermute(own, "tp", down)
    blocks, steps, state = [[right], [left], [own]], (tp_size - 1, 1, 0), None
    seen = [(0, own), (tp_size - 1, right), (1, left)]
    for far in range(2, tp_size // 2):
        next_right = lax.ppermute(right, "tp", up)
        next_left = lax.ppermute(left, "tp", down)
        state = attention(blocks=blocks, steps=steps, state=state)
        right, state = lax.optimization_barrier((next_right, state))
        left = next_left
        blocks, steps = [[right], [left]], (tp_size - far, far)
        seen += [(tp_size - far, right), (far, left)]
    cut = cols * LANES
    last = [lax.ppermute(right[:cut], "tp", up), lax.ppermute(left[cut:], "tp", down)]
    state = attention(blocks=blocks, steps=steps, state=state)
    attn_out, turned = attention(
        blocks=[last],
        steps=(tp_size // 2,),
        state=state,
        absorb_v=absorb_v,
        seen=tuple(seen),
    )
    return attn_out, turned.T


def solution(mesh):
    placed = (
        P("dp", "tp"),
        P("tp", None),
        P(),
        P("dp", "tp"),
        P("dp", "tp"),
        P("tp", None, None),
        P("tp", None, None),
        P("dp", None, None),
        P("dp", None, None),
        P("dp", None),
        P("dp"),
    )
    return jax.shard_map(
        shards,
        mesh=mesh,
        in_specs=placed,
        out_specs=(P("dp", "tp"), P("dp", None)),
        check_vma=False,
    )
```

```python
import functools
import math

import jax
import jax.numpy as jnp
from jax import lax
from jax.experimental import pallas as pl
from jax.experimental.pallas import tpu as pltpu
from jax.sharding import PartitionSpec as P

BF16 = jnp.bfloat16
F32 = jnp.float32
MASKED = -1e30
LANES = 128


def turn_tables(position, half_width):
    frequency = 10000.0 ** (-jnp.arange(half_width, dtype=F32) / half_width)
    angles = position[:, None].astype(F32) * frequency[None, :]
    return jnp.cos(angles), jnp.sin(angles)


VMEM = pl.BlockSpec(memory_space=pltpu.VMEM)
SMEM = pl.BlockSpec(memory_space=pltpu.SMEM)
SMALL = pltpu.CompilerParams(vmem_limit_bytes=4 << 20)


def deal_body(place_ref, part_ref, keep_ref, *gives):
    rows = keep_ref.shape[0]
    keep_ref[...] = part_ref[pl.ds(pl.multiple_of(place_ref[0] * rows, rows), rows), :]
    for i, give_ref in enumerate(gives):
        other = pl.multiple_of(place_ref[1 + i] * rows, rows)
        give_ref[...] = part_ref[pl.ds(other, rows), :].astype(BF16)


def deal(place, part, members):
    rows, width = part.shape[0] // members, part.shape[1]
    return pl.pallas_call(
        deal_body,
        out_shape=(jax.ShapeDtypeStruct((rows, width), F32),)
        + (jax.ShapeDtypeStruct((rows, width), BF16),) * (members - 1),
        in_specs=[SMEM, VMEM],
        out_specs=(VMEM,) * members,
        compiler_params=SMALL,
        name="deal",
    )(place, part)


def finish_body(kept_ref, gain_ref, cos_ref, sin_ref, *rest):
    out_ref = rest[-1]
    width = gain_ref.shape[1]
    raw = kept_ref[...]
    for got_ref in rest[:-1]:
        raw = raw + got_ref[...].astype(F32)
    compressed = raw[:, :width]
    mean_square = jnp.mean(compressed * compressed, axis=1, keepdims=True)
    latent = (compressed * lax.rsqrt(mean_square + 1e-06) * gain_ref[...]).astype(BF16)
    half = cos_ref.shape[1]
    first, second = raw[:, width : width + half], raw[:, width + half :]
    cosine, sine = cos_ref[...], sin_ref[...]
    turned = jnp.concatenate(
        [first * cosine - second * sine, second * cosine + first * sine], axis=1
    )
    rows = raw.shape[0]
    for c in range(width // LANES):
        out_ref[c * rows : (c + 1) * rows, :] = latent[:, c * LANES : (c + 1) * LANES]
    out_ref[width // LANES * rows :, :] = jnp.concatenate(
        [turned[: rows // 2], turned[rows // 2 :]], axis=1
    ).astype(BF16)


def finish_latents(kept, gain, cosine, sine, got):
    rows, width = kept.shape[0], gain.shape[1]
    return pl.pallas_call(
        finish_body,
        out_shape=jax.ShapeDtypeStruct((width // LANES * rows + rows // 2, LANES), BF16),
        in_specs=[VMEM] * (4 + len(got)),
        out_specs=VMEM,
        compiler_params=SMALL,
        name="finish_latents",
    )(kept, gain, cosine, sine, *got)


def plan_body(owner_ref, slot_ref, want_ref, pick_ref):
    reqs, pages = owner_ref.shape
    for owner in range(want_ref.shape[0]):
        want_ref[owner, 0, 0] = -1
        want_ref[owner, 0, 1] = -1
    for r in range(reqs):
        for i in range(pages):
            owner = owner_ref[r, i]
            rank = jnp.where(want_ref[owner, 0, 0] < 0, 0, 1)
            want_ref[owner, 0, rank] = slot_ref[r, i]
            pick_ref[r * pages + i] = 2 * owner + rank


def plan(owners, slots, dp_size):
    smem = pl.BlockSpec(memory_space=pltpu.SMEM)
    return pl.pallas_call(
        plan_body,
        out_shape=(
            jax.ShapeDtypeStruct((dp_size, 1, 2), jnp.int32),
            jax.ShapeDtypeStruct((owners.size,), jnp.int32),
        ),
        in_specs=[smem, smem],
        out_specs=(smem, smem),
        name="plan",
    )(owners, slots)


def gather_body(ids_ref, pages_ref, out_ref):
    last = pages_ref.shape[0] - 1
    for i in range(ids_ref.shape[0]):
        for j in range(2):
            out_ref[i, j] = pages_ref[jnp.clip(ids_ref[i, 0, j], 0, last)]


def gather_pages(ids, pages):
    return pl.pallas_call(
        gather_body,
        out_shape=jax.ShapeDtypeStruct((ids.shape[0], 2) + pages.shape[1:], pages.dtype),
        in_specs=[
            pl.BlockSpec(memory_space=pltpu.SMEM),
            pl.BlockSpec(memory_space=pltpu.VMEM),
        ],
        out_specs=pl.BlockSpec(memory_space=pltpu.VMEM),
        compiler_params=pltpu.CompilerParams(vmem_limit_bytes=4 << 20),
        name="gather_pages",
    )(ids, pages)


def select_body(pick_ref, fetched_ref, fresh_ref, out_ref, *, cols):
    out_ref[(2 * cols + 1) * LANES :, :] = fresh_ref[...]
    entries = pick_ref.shape[0]
    per_req = entries // 2
    rows = 2 * fetched_ref.shape[1]
    width = cols * LANES
    for i in range(per_req // 2):
        tails = []
        for r in range(2):
            first = pick_ref[r * per_req + 2 * i]
            second = pick_ref[r * per_req + 2 * i + 1]
            both = jnp.concatenate(
                [fetched_ref[first].astype(F32), fetched_ref[second].astype(F32)], axis=0
            )
            at = r * LANES + i * rows
            for c in range(cols):
                out_ref[pl.ds(c * 2 * LANES + at, rows), :] = both[
                    :, c * LANES : (c + 1) * LANES
                ].astype(BF16)
            tails.append(both[:, width:])
        out_ref[pl.ds(cols * 2 * LANES + i * rows, rows), :] = jnp.concatenate(
            tails, axis=1
        ).astype(BF16)


def select_pages(pick, fetched, fresh, cols):
    return pl.pallas_call(
        functools.partial(select_body, cols=cols),
        out_shape=jax.ShapeDtypeStruct(((2 * cols + 1) * LANES + fresh.shape[0], LANES), BF16),
        in_specs=[
            SMEM,
            VMEM,
            VMEM,
        ],
        out_specs=VMEM,
        compiler_params=SMALL,
        name="select_pages",
    )(pick, fetched, fresh)


def query_body(nope_ref, rope_ref, absorb_ref, out_ref):
    rows = nope_ref.shape[0]
    half = rows // 2
    heads, nope, width = absorb_ref.shape
    side = LANES // 2
    for p in range(heads // 2):
        rope = rope_ref[:, p * LANES : (p + 1) * LANES].T
        for h in range(2):
            n = 2 * p + h
            latent = lax.dot_general(
                absorb_ref[n],
                nope_ref[:, n * nope : (n + 1) * nope],
                (((0,), (1,)), ((), ())),
                preferred_element_type=F32,
            ).astype(BF16)
            at = slice(h * LANES, (h + 1) * LANES)
            for r in range(2):
                out_ref[p, r, :width, at] = latent[:, r * half : (r + 1) * half]
                put, skip = width + r * side, width + (1 - r) * side
                out_ref[p, r, put : put + side, at] = rope[
                    h * side : (h + 1) * side, r * half : (r + 1) * half
                ]
                out_ref[p, r, skip : skip + side, at] = jnp.zeros((side, LANES), BF16)


def queries(q_nope, q_rope, absorb_k):
    rows = q_nope.shape[0]
    heads, _, width = absorb_k.shape
    vmem = pl.BlockSpec(memory_space=pltpu.VMEM)
    return pl.pallas_call(
        query_body,
        out_shape=jax.ShapeDtypeStruct((heads // 2, 2, width + LANES, rows), BF16),
        in_specs=[vmem] * 3,
        out_specs=vmem,
        compiler_params=pltpu.CompilerParams(vmem_limit_bytes=16 << 20),
        name="queries",
    )(q_nope, q_rope, absorb_k)


def lay_block(parts, b, r, step, origin_ref, prefix_ref, keys_ref, values_ref, bias_ref, page, split):
    width = values_ref.shape[0]
    at = slice(b * LANES, (b + 1) * LANES)
    starts = []
    for part in parts:
        starts += [(part, i) for i in range(0, part.shape[0], LANES)]
    for c in range(width // LANES):
        ref, low = starts[2 * c + r]
        tile = ref[low : low + LANES, :]
        keys_ref[at, c * LANES : (c + 1) * LANES] = tile
        values_ref[c * LANES : (c + 1) * LANES, at] = tile.T
    ref, low = starts[2 * (width // LANES)]
    keys_ref[at, width:] = ref[low : low + LANES, :]
    place = lax.broadcasted_iota(jnp.int32, (LANES, LANES), 0)
    position = place // split * page + origin_ref[step] * split + place % split
    bias_ref[at, :] = jnp.where(position < prefix_ref[r], 0.0, MASKED)


def join_new(tails, origin_ref, new_ref):
    for ref, low, step in tails:
        rows = (ref.shape[0] - low) * 2 // 9
        first = pl.multiple_of(origin_ref[step] * rows, rows)
        for c in range(4):
            new_ref[pl.ds(first, rows), c * LANES : (c + 1) * LANES] = ref[
                low + c * rows : low + (c + 1) * rows, :
            ]
        turned = ref[low + 4 * rows :, :]
        half = rows // 2
        for h in range(2):
            place = pl.multiple_of(first + h * half, half)
            new_ref[pl.ds(place, half), 4 * LANES :] = turned[
                :, h * LANES // 2 : (h + 1) * LANES // 2
            ]


def lay_new(new_ref, b, r, keys_ref, values_ref, bias_ref):
    width = values_ref.shape[0]
    side = LANES // 2
    at = slice(b * LANES, (b + 1) * LANES)
    rows = slice(r * LANES, (r + 1) * LANES)
    for c in range(width // LANES):
        tile = new_ref[rows, c * LANES : (c + 1) * LANES]
        keys_ref[at, c * LANES : (c + 1) * LANES] = tile
        values_ref[c * LANES : (c + 1) * LANES, at] = tile.T
    put, skip = width + r * side, width + (1 - r) * side
    keys_ref[at, put : put + side] = new_ref[rows, width:]
    keys_ref[at, skip : skip + side] = jnp.zeros((LANES, side), BF16)
    place = lax.broadcasted_iota(jnp.int32, (LANES, LANES), 0)
    token = lax.broadcasted_iota(jnp.int32, (LANES, LANES), 1)
    bias_ref[at, :] = jnp.where(place <= token, 0.0, MASKED)


def attend_body(*refs, pieces, steps, seen_steps, full_width, first, last, factor, page, split):
    refs = list(refs)
    origin_ref, prefix_ref, query_ref = [refs.pop(0) for _ in range(3)]
    blocks = [[refs.pop(0) for _ in range(n)] for n in pieces]
    if not first:
        acc_in, stat_in = refs.pop(0), refs.pop(0)
    if last:
        seen = [refs.pop(0) for _ in seen_steps]
        absorb_ref, out_ref, turned_ref, new_ref = [refs.pop(0) for _ in range(3)] + [refs.pop()]
        low = (full_width // LANES * 2 - 1) * LANES
        tails = [(ref, low, step) for ref, step in zip(seen, seen_steps)]
        cut = blocks[0][0].shape[0]
        join_new(tails + [(blocks[0][1], low - cut, steps[0])], origin_ref, new_ref)
    else:
        acc_out, stat_out = refs.pop(0), refs.pop(0)
    keys_ref, values_ref, bias_ref = refs
    pairs, reqs, full, lanes = query_ref.shape

    def score(r, k):
        s = jnp.dot(keys_ref[r], query_ref[k, r], preferred_element_type=F32)
        bias = bias_ref[r]
        return s + jnp.concatenate([bias, bias], axis=1)

    def soften(r, k, s):
        top = jnp.max(s, axis=0, keepdims=True)
        if not first:
            old_top = stat_in[k, r, 0:1, :]
            top = jnp.maximum(top, old_top)
        expo = jnp.exp2((s - top) * factor)
        total = jnp.sum(expo, axis=0, keepdims=True)
        return expo.astype(BF16), top, total

    def finish(r, k, probs, top, total):
        acc = jnp.dot(values_ref[r], probs, preferred_element_type=F32)
        if not first:
            alpha = jnp.exp2((stat_in[k, r, 0:1, :] - top) * factor)
            total = total + alpha * stat_in[k, r, 1:2, :]
            acc = acc + alpha * acc_in[k, r].astype(F32)
        if last:
            latent = (acc * (1.0 / total)).astype(BF16)
            vdim = absorb_ref.shape[2]
            tokens = lanes // 2
            for h in range(2):
                n = 2 * k + h
                out_ref[r * tokens : (r + 1) * tokens, n * vdim : (n + 1) * vdim] = lax.dot_general(
                    latent[:, h * tokens : (h + 1) * tokens],
                    absorb_ref[n],
                    (((0,), (0,)), ((), ())),
                    preferred_element_type=F32,
                ).astype(BF16)
        else:
            acc_out[k, r] = acc.astype(BF16)
            stat_out[k, r, 0:1, :] = top
            stat_out[k, r, 1:2, :] = total

    for r in range(reqs):
        for b, parts in enumerate(blocks):
            lay_block(
                parts, b, r, steps[b], origin_ref, prefix_ref,
                keys_ref.at[r], values_ref.at[r], bias_ref.at[r], page, split,
            )
        if last:
            lay_new(new_ref, len(blocks), r, keys_ref.at[r], values_ref.at[r], bias_ref.at[r])
            own = slice(r * LANES, (r + 1) * LANES)
            turned_ref[: full - LANES, own] = values_ref[r, :, len(blocks) * LANES :]
            turned_ref[full - LANES :, own] = new_ref[own, full - LANES :].T
    order = [(r, k) for r in range(reqs) for k in range(pairs)]
    count = len(order)
    scores, probs = {}, {}
    for i in range(count + 2):
        if i < count:
            scores[i] = score(*order[i])
        if 0 <= i - 1 < count:
            probs[i - 1] = soften(*order[i - 1], scores.pop(i - 1))
        if 0 <= i - 2 < count:
            finish(*order[i - 2], *probs.pop(i - 2))


def attend(
    query, blocks, steps, origins, prefix_len, factor, page, split, state=None, absorb_v=None, seen=()
):
    pairs, reqs, full, lanes = query.shape
    width = full - LANES
    first, last = state is None, absorb_v is not None
    args = [query] + [part for parts in blocks for part in parts]
    aliases = {}
    if not first:
        if not last:
            aliases = {2 + len(args): 0, 3 + len(args): 1}
        args += list(state)
    if last:
        args += [block for _, block in seen] + [absorb_v]
        vdim = absorb_v.shape[2]
        out_shape = (
            jax.ShapeDtypeStruct((reqs * lanes // 2, 2 * pairs * vdim), BF16),
            jax.ShapeDtypeStruct((width + LANES // 2, reqs * lanes // 2), BF16),
        )
    else:
        out_shape = (
            jax.ShapeDtypeStruct((pairs, reqs, width, lanes), BF16),
            jax.ShapeDtypeStruct((pairs, reqs, 8, lanes), F32),
        )
    keys = (len(blocks) + last) * LANES
    return pl.pallas_call(
        functools.partial(
            attend_body,
            pieces=tuple(len(parts) for parts in blocks),
            steps=steps,
            seen_steps=tuple(step for step, _ in seen),
            full_width=full,
            first=first,
            last=last,
            factor=factor,
            page=page,
            split=split,
        ),
        out_shape=out_shape,
        in_specs=[SMEM, SMEM] + [VMEM] * len(args),
        out_specs=(VMEM, VMEM),
        input_output_aliases=aliases,
        scratch_shapes=[
            pltpu.VMEM((reqs, keys, full), BF16),
            pltpu.VMEM((reqs, width, keys), BF16),
            pltpu.VMEM((reqs, keys, LANES), F32),
        ]
        + [pltpu.VMEM((reqs * lanes // 2, width + LANES // 2), BF16)] * last,
        compiler_params=pltpu.CompilerParams(vmem_limit_bytes=16 << 20),
        cost_estimate=pl.CostEstimate(
            flops=2 * pairs * reqs * lanes * keys * (full + width),
            bytes_accessed=2 * pairs * reqs * lanes * (full + 2 * width),
            transcendentals=pairs * reqs * lanes * keys,
        ),
        name="attend",
    )(origins, prefix_len, *args)


def shards(
    hidden_in,
    kv_down,
    latent_gain,
    q_nope,
    q_rope,
    absorb_k,
    absorb_v,
    store,
    page_owner,
    page_slot,
    prefix_len,
):
    rows = hidden_in.shape[0]
    reqs = prefix_len.shape[0]
    new_len = rows // reqs
    kv_rank = latent_gain.shape[0]
    lat_width = kv_down.shape[1]
    nope_width = absorb_k.shape[1]
    rope_width = lat_width - kv_rank
    page = store.shape[1]
    dp_size = lax.axis_size("dp")
    tp_size = lax.axis_size("tp")
    z = lax.axis_index("tp")
    split = page // tp_size
    cols = kv_rank // LANES

    place = jnp.stack([z ^ i for i in range(tp_size)]).astype(jnp.int32)
    origins = ((z + jnp.arange(tp_size, dtype=jnp.int32)) % tp_size).astype(jnp.int32)
    own_rows = rows // tp_size
    token = z * own_rows + jnp.arange(own_rows, dtype=jnp.int32)
    position = jnp.where(token // new_len == 0, prefix_len[0], prefix_len[1]) + token % new_len
    piece = lax.dynamic_slice_in_dim(store, z * split, split, axis=1)

    def swap(given, far):
        return lax.ppermute(given, "tp", [(i, i ^ far) for i in range(tp_size)])

    want, pick = plan(page_owner[:, :, 0], page_slot, dp_size)
    asked = lax.all_to_all(want, "dp", split_axis=0, concat_axis=0, tiled=True)

    reply = gather_pages(asked, piece)
    reply, hidden_in, place, position = lax.optimization_barrier(
        (reply, hidden_in, place, position)
    )
    fetched = lax.all_to_all(reply, "dp", split_axis=0, concat_axis=0, tiled=True)

    cosine, sine = turn_tables(position, rope_width // 2)
    gain = latent_gain[None, :]
    part = jnp.dot(hidden_in, kv_down, preferred_element_type=F32)
    kept, *gives = deal(place, part, tp_size)
    got = [swap(given, i + 1) for i, given in enumerate(gives)]
    fresh = finish_latents(kept, gain, cosine, sine, got)
    fetched, fresh, q_nope = lax.optimization_barrier((fetched, fresh, q_nope))

    query = queries(q_nope, q_rope, absorb_k)
    attention = functools.partial(
        attend,
        query,
        origins=origins,
        prefix_len=prefix_len,
        factor=math.log2(math.e) / math.sqrt(nope_width + rope_width),
        page=page,
        split=split,
    )
    up = [(i, (i + 1) % tp_size) for i in range(tp_size)]
    down = [(i, (i - 1) % tp_size) for i in range(tp_size)]
    own = select_pages(pick, fetched.reshape(2 * dp_size, split, lat_width), fresh, cols)
    right, left = lax.ppermute(own, "tp", up), lax.ppermute(own, "tp", down)
    state = attention(blocks=[[own]], steps=(0,))
    right, left, state = lax.optimization_barrier((right, left, state))
    blocks, steps = [[right], [left]], (tp_size - 1, 1)
    seen = [(0, own), (tp_size - 1, right), (1, left)]
    for far in range(2, tp_size // 2):
        next_right = lax.ppermute(right, "tp", up)
        next_left = lax.ppermute(left, "tp", down)
        state = attention(blocks=blocks, steps=steps, state=state)
        right, state = lax.optimization_barrier((next_right, state))
        left = next_left
        blocks, steps = [[right], [left]], (tp_size - far, far)
        seen += [(tp_size - far, right), (far, left)]
    cut = (2 * cols + 1) * 2 // 3 * LANES
    last = [lax.ppermute(right[:cut], "tp", up), lax.ppermute(left[cut:], "tp", down)]
    state = attention(blocks=blocks, steps=steps, state=state)
    attn_out, turned = attention(
        blocks=[last],
        steps=(tp_size // 2,),
        state=state,
        absorb_v=absorb_v,
        seen=tuple(seen),
    )
    return attn_out, turned.T


def solution(mesh):
    placed = (
        P("dp", "tp"),
        P("tp", None),
        P(),
        P("dp", "tp"),
        P("dp", "tp"),
        P("tp", None, None),
        P("tp", None, None),
        P("dp", None, None),
        P("dp", None, None),
        P("dp", None),
        P("dp"),
    )
    return jax.shard_map(
        shards,
        mesh=mesh,
        in_specs=placed,
        out_specs=(P("dp", "tp"), P("dp", None)),
        check_vma=False,
    )
```

```python
import functools
import math

import jax
import jax.numpy as jnp
from jax import lax
from jax.experimental import pallas as pl
from jax.experimental.pallas import tpu as pltpu
from jax.sharding import PartitionSpec as P

BF16 = jnp.bfloat16
F32 = jnp.float32
MASKED = -1e30
LANES = 128


def turn_tables(position, half_width):
    frequency = 10000.0 ** (-jnp.arange(half_width, dtype=F32) / half_width)
    angles = position[:, None].astype(F32) * frequency[None, :]
    return jnp.cos(angles), jnp.sin(angles)


VMEM = pl.BlockSpec(memory_space=pltpu.VMEM)
SMEM = pl.BlockSpec(memory_space=pltpu.SMEM)
SMALL = pltpu.CompilerParams(vmem_limit_bytes=4 << 20)


def deal_body(place_ref, part_ref, keep_ref, *gives):
    rows = keep_ref.shape[0]
    keep_ref[...] = part_ref[pl.ds(pl.multiple_of(place_ref[0] * rows, rows), rows), :]
    for i, give_ref in enumerate(gives):
        other = pl.multiple_of(place_ref[1 + i] * rows, rows)
        give_ref[...] = part_ref[pl.ds(other, rows), :].astype(BF16)


def deal(place, part, members):
    rows, width = part.shape[0] // members, part.shape[1]
    return pl.pallas_call(
        deal_body,
        out_shape=(jax.ShapeDtypeStruct((rows, width), F32),)
        + (jax.ShapeDtypeStruct((rows, width), BF16),) * (members - 1),
        in_specs=[SMEM, VMEM],
        out_specs=(VMEM,) * members,
        compiler_params=SMALL,
        name="deal",
    )(place, part)


def finish_body(kept_ref, gain_ref, cos_ref, sin_ref, *rest):
    out_ref = rest[-1]
    width = gain_ref.shape[1]
    raw = kept_ref[...]
    for got_ref in rest[:-1]:
        raw = raw + got_ref[...].astype(F32)
    compressed = raw[:, :width]
    mean_square = jnp.mean(compressed * compressed, axis=1, keepdims=True)
    latent = (compressed * lax.rsqrt(mean_square + 1e-06) * gain_ref[...]).astype(BF16)
    half = cos_ref.shape[1]
    first, second = raw[:, width : width + half], raw[:, width + half :]
    cosine, sine = cos_ref[...], sin_ref[...]
    turned = jnp.concatenate(
        [first * cosine - second * sine, second * cosine + first * sine], axis=1
    )
    rows = raw.shape[0]
    for c in range(width // LANES):
        out_ref[c * rows : (c + 1) * rows, :] = latent[:, c * LANES : (c + 1) * LANES]
    out_ref[width // LANES * rows :, :] = jnp.concatenate(
        [turned[: rows // 2], turned[rows // 2 :]], axis=1
    ).astype(BF16)


def finish_latents(kept, gain, cosine, sine, got):
    rows, width = kept.shape[0], gain.shape[1]
    return pl.pallas_call(
        finish_body,
        out_shape=jax.ShapeDtypeStruct((width // LANES * rows + rows // 2, LANES), BF16),
        in_specs=[VMEM] * (4 + len(got)),
        out_specs=VMEM,
        compiler_params=SMALL,
        name="finish_latents",
    )(kept, gain, cosine, sine, *got)


def plan_body(owner_ref, slot_ref, want_ref, pick_ref):
    reqs, pages = owner_ref.shape
    for owner in range(want_ref.shape[0]):
        want_ref[owner, 0, 0] = -1
        want_ref[owner, 0, 1] = -1
    for r in range(reqs):
        for i in range(pages):
            owner = owner_ref[r, i]
            rank = jnp.where(want_ref[owner, 0, 0] < 0, 0, 1)
            want_ref[owner, 0, rank] = slot_ref[r, i]
            pick_ref[r * pages + i] = 2 * owner + rank


def plan(owners, slots, dp_size):
    smem = pl.BlockSpec(memory_space=pltpu.SMEM)
    return pl.pallas_call(
        plan_body,
        out_shape=(
            jax.ShapeDtypeStruct((dp_size, 1, 2), jnp.int32),
            jax.ShapeDtypeStruct((owners.size,), jnp.int32),
        ),
        in_specs=[smem, smem],
        out_specs=(smem, smem),
        name="plan",
    )(owners, slots)


def gather_body(ids_ref, pages_ref, out_ref):
    last = pages_ref.shape[0] - 1
    for i in range(ids_ref.shape[0]):
        for j in range(2):
            out_ref[i, j] = pages_ref[jnp.clip(ids_ref[i, 0, j], 0, last)]


def gather_pages(ids, pages):
    return pl.pallas_call(
        gather_body,
        out_shape=jax.ShapeDtypeStruct((ids.shape[0], 2) + pages.shape[1:], pages.dtype),
        in_specs=[
            pl.BlockSpec(memory_space=pltpu.SMEM),
            pl.BlockSpec(memory_space=pltpu.VMEM),
        ],
        out_specs=pl.BlockSpec(memory_space=pltpu.VMEM),
        compiler_params=pltpu.CompilerParams(vmem_limit_bytes=4 << 20),
        name="gather_pages",
    )(ids, pages)


def select_body(pick_ref, fetched_ref, fresh_ref, out_ref, *, cols):
    out_ref[(2 * cols + 1) * LANES :, :] = fresh_ref[...]
    entries = pick_ref.shape[0]
    per_req = entries // 2
    rows = 2 * fetched_ref.shape[1]
    width = cols * LANES
    for i in range(per_req // 2):
        tails = []
        for r in range(2):
            first = pick_ref[r * per_req + 2 * i]
            second = pick_ref[r * per_req + 2 * i + 1]
            both = jnp.concatenate(
                [fetched_ref[first].astype(F32), fetched_ref[second].astype(F32)], axis=0
            )
            at = r * LANES + i * rows
            for c in range(cols):
                out_ref[pl.ds(c * 2 * LANES + at, rows), :] = both[
                    :, c * LANES : (c + 1) * LANES
                ].astype(BF16)
            tails.append(both[:, width:])
        out_ref[pl.ds(cols * 2 * LANES + i * rows, rows), :] = jnp.concatenate(
            tails, axis=1
        ).astype(BF16)


def select_pages(pick, fetched, fresh, cols):
    return pl.pallas_call(
        functools.partial(select_body, cols=cols),
        out_shape=jax.ShapeDtypeStruct(((2 * cols + 1) * LANES + fresh.shape[0], LANES), BF16),
        in_specs=[
            SMEM,
            VMEM,
            VMEM,
        ],
        out_specs=VMEM,
        compiler_params=SMALL,
        name="select_pages",
    )(pick, fetched, fresh)


def query_body(nope_ref, rope_ref, absorb_ref, out_ref):
    rows = nope_ref.shape[0]
    half = rows // 2
    heads, nope, width = absorb_ref.shape
    side = LANES // 2
    for p in range(heads // 2):
        rope = rope_ref[:, p * LANES : (p + 1) * LANES].T
        for h in range(2):
            n = 2 * p + h
            latent = lax.dot_general(
                absorb_ref[n],
                nope_ref[:, n * nope : (n + 1) * nope],
                (((0,), (1,)), ((), ())),
                preferred_element_type=F32,
            ).astype(BF16)
            at = slice(h * LANES, (h + 1) * LANES)
            for r in range(2):
                out_ref[p, r, :width, at] = latent[:, r * half : (r + 1) * half]
                put, skip = width + r * side, width + (1 - r) * side
                out_ref[p, r, put : put + side, at] = rope[
                    h * side : (h + 1) * side, r * half : (r + 1) * half
                ]
                out_ref[p, r, skip : skip + side, at] = jnp.zeros((side, LANES), BF16)


def queries(q_nope, q_rope, absorb_k):
    rows = q_nope.shape[0]
    heads, _, width = absorb_k.shape
    vmem = pl.BlockSpec(memory_space=pltpu.VMEM)
    return pl.pallas_call(
        query_body,
        out_shape=jax.ShapeDtypeStruct((heads // 2, 2, width + LANES, rows), BF16),
        in_specs=[vmem] * 3,
        out_specs=vmem,
        compiler_params=pltpu.CompilerParams(vmem_limit_bytes=16 << 20),
        name="queries",
    )(q_nope, q_rope, absorb_k)


def lay_block(parts, b, r, step, origin_ref, prefix_ref, keys_ref, values_ref, bias_ref, page, split):
    width = values_ref.shape[0]
    at = slice(b * LANES, (b + 1) * LANES)
    starts = []
    for part in parts:
        starts += [(part, i) for i in range(0, part.shape[0], LANES)]
    for c in range(width // LANES):
        ref, low = starts[2 * c + r]
        tile = ref[low : low + LANES, :]
        keys_ref[at, c * LANES : (c + 1) * LANES] = tile
        values_ref[c * LANES : (c + 1) * LANES, at] = tile.T
    ref, low = starts[2 * (width // LANES)]
    keys_ref[at, width:] = ref[low : low + LANES, :]
    place = lax.broadcasted_iota(jnp.int32, (LANES, LANES), 0)
    position = place // split * page + origin_ref[step] * split + place % split
    bias_ref[at, :] = jnp.where(position < prefix_ref[r], 0.0, MASKED)


def join_new(tails, origin_ref, new_ref):
    for ref, low, step in tails:
        rows = (ref.shape[0] - low) * 2 // 9
        first = pl.multiple_of(origin_ref[step] * rows, rows)
        for c in range(4):
            new_ref[pl.ds(first, rows), c * LANES : (c + 1) * LANES] = ref[
                low + c * rows : low + (c + 1) * rows, :
            ]
        turned = ref[low + 4 * rows :, :]
        half = rows // 2
        for h in range(2):
            place = pl.multiple_of(first + h * half, half)
            new_ref[pl.ds(place, half), 4 * LANES :] = turned[
                :, h * LANES // 2 : (h + 1) * LANES // 2
            ]


def lay_new(new_ref, b, r, keys_ref, values_ref, bias_ref):
    width = values_ref.shape[0]
    side = LANES // 2
    at = slice(b * LANES, (b + 1) * LANES)
    rows = slice(r * LANES, (r + 1) * LANES)
    for c in range(width // LANES):
        tile = new_ref[rows, c * LANES : (c + 1) * LANES]
        keys_ref[at, c * LANES : (c + 1) * LANES] = tile
        values_ref[c * LANES : (c + 1) * LANES, at] = tile.T
    put, skip = width + r * side, width + (1 - r) * side
    keys_ref[at, put : put + side] = new_ref[rows, width:]
    keys_ref[at, skip : skip + side] = jnp.zeros((LANES, side), BF16)
    place = lax.broadcasted_iota(jnp.int32, (LANES, LANES), 0)
    token = lax.broadcasted_iota(jnp.int32, (LANES, LANES), 1)
    bias_ref[at, :] = jnp.where(place <= token, 0.0, MASKED)


def attend_body(*refs, pieces, steps, seen_steps, full_width, first, last, factor, page, split):
    refs = list(refs)
    origin_ref, prefix_ref, query_ref = [refs.pop(0) for _ in range(3)]
    blocks = [[refs.pop(0) for _ in range(n)] for n in pieces]
    if not first:
        acc_in, stat_in = refs.pop(0), refs.pop(0)
    if last:
        seen = [refs.pop(0) for _ in seen_steps]
        absorb_ref, out_ref, turned_ref, new_ref = [refs.pop(0) for _ in range(3)] + [refs.pop()]
        low = (full_width // LANES * 2 - 1) * LANES
        tails = [(ref, low, step) for ref, step in zip(seen, seen_steps)]
        cut = blocks[0][0].shape[0]
        join_new(tails + [(blocks[0][1], low - cut, steps[0])], origin_ref, new_ref)
    else:
        acc_out, stat_out = refs.pop(0), refs.pop(0)
    keys_ref, values_ref, bias_ref = refs
    pairs, reqs, full, lanes = query_ref.shape

    def score(r, k):
        s = jnp.dot(keys_ref[r], query_ref[k, r], preferred_element_type=F32)
        bias = bias_ref[r]
        return s + jnp.concatenate([bias, bias], axis=1)

    def soften(r, k, s):
        top = jnp.max(s, axis=0, keepdims=True)
        if not first:
            old_top = stat_in[k, r, 0:1, :]
            top = jnp.maximum(top, old_top)
        expo = jnp.exp2((s - top) * factor)
        total = jnp.sum(expo, axis=0, keepdims=True)
        return expo.astype(BF16), top, total

    def finish(r, k, probs, top, total):
        acc = jnp.dot(values_ref[r], probs, preferred_element_type=F32)
        if not first:
            alpha = jnp.exp2((stat_in[k, r, 0:1, :] - top) * factor)
            total = total + alpha * stat_in[k, r, 1:2, :]
            acc = acc + alpha * acc_in[k, r].astype(F32)
        if last:
            latent = (acc * (1.0 / total)).astype(BF16)
            vdim = absorb_ref.shape[2]
            tokens = lanes // 2
            for h in range(2):
                n = 2 * k + h
                out_ref[r * tokens : (r + 1) * tokens, n * vdim : (n + 1) * vdim] = lax.dot_general(
                    latent[:, h * tokens : (h + 1) * tokens],
                    absorb_ref[n],
                    (((0,), (0,)), ((), ())),
                    preferred_element_type=F32,
                ).astype(BF16)
        else:
            acc_out[k, r] = acc.astype(BF16)
            stat_out[k, r, 0:1, :] = top
            stat_out[k, r, 1:2, :] = total

    for r in range(reqs):
        for b, parts in enumerate(blocks):
            lay_block(
                parts, b, r, steps[b], origin_ref, prefix_ref,
                keys_ref.at[r], values_ref.at[r], bias_ref.at[r], page, split,
            )
        if last:
            lay_new(new_ref, len(blocks), r, keys_ref.at[r], values_ref.at[r], bias_ref.at[r])
            own = slice(r * LANES, (r + 1) * LANES)
            turned_ref[: full - LANES, own] = values_ref[r, :, len(blocks) * LANES :]
            turned_ref[full - LANES :, own] = new_ref[own, full - LANES :].T
    order = [(r, k) for r in range(reqs) for k in range(pairs)]
    count = len(order)
    scores, probs = {}, {}
    for i in range(count + 2):
        if i < count:
            scores[i] = score(*order[i])
        if 0 <= i - 1 < count:
            probs[i - 1] = soften(*order[i - 1], scores.pop(i - 1))
        if 0 <= i - 2 < count:
            finish(*order[i - 2], *probs.pop(i - 2))


def attend(
    query, blocks, steps, origins, prefix_len, factor, page, split, state=None, absorb_v=None, seen=()
):
    pairs, reqs, full, lanes = query.shape
    width = full - LANES
    first, last = state is None, absorb_v is not None
    args = [query] + [part for parts in blocks for part in parts]
    aliases = {}
    if not first:
        if not last:
            aliases = {2 + len(args): 0, 3 + len(args): 1}
        args += list(state)
    if last:
        args += [block for _, block in seen] + [absorb_v]
        vdim = absorb_v.shape[2]
        out_shape = (
            jax.ShapeDtypeStruct((reqs * lanes // 2, 2 * pairs * vdim), BF16),
            jax.ShapeDtypeStruct((width + LANES // 2, reqs * lanes // 2), BF16),
        )
    else:
        out_shape = (
            jax.ShapeDtypeStruct((pairs, reqs, width, lanes), BF16),
            jax.ShapeDtypeStruct((pairs, reqs, 8, lanes), F32),
        )
    keys = (len(blocks) + last) * LANES
    return pl.pallas_call(
        functools.partial(
            attend_body,
            pieces=tuple(len(parts) for parts in blocks),
            steps=steps,
            seen_steps=tuple(step for step, _ in seen),
            full_width=full,
            first=first,
            last=last,
            factor=factor,
            page=page,
            split=split,
        ),
        out_shape=out_shape,
        in_specs=[SMEM, SMEM] + [VMEM] * len(args),
        out_specs=(VMEM, VMEM),
        input_output_aliases=aliases,
        scratch_shapes=[
            pltpu.VMEM((reqs, keys, full), BF16),
            pltpu.VMEM((reqs, width, keys), BF16),
            pltpu.VMEM((reqs, keys, LANES), F32),
        ]
        + [pltpu.VMEM((reqs * lanes // 2, width + LANES // 2), BF16)] * last,
        compiler_params=pltpu.CompilerParams(vmem_limit_bytes=16 << 20),
        cost_estimate=pl.CostEstimate(
            flops=2 * pairs * reqs * lanes * keys * (full + width),
            bytes_accessed=2 * pairs * reqs * lanes * (full + 2 * width),
            transcendentals=pairs * reqs * lanes * keys,
        ),
        name="attend",
    )(origins, prefix_len, *args)


def shards(
    hidden_in,
    kv_down,
    latent_gain,
    q_nope,
    q_rope,
    absorb_k,
    absorb_v,
    store,
    page_owner,
    page_slot,
    prefix_len,
):
    rows = hidden_in.shape[0]
    reqs = prefix_len.shape[0]
    new_len = rows // reqs
    kv_rank = latent_gain.shape[0]
    lat_width = kv_down.shape[1]
    nope_width = absorb_k.shape[1]
    rope_width = lat_width - kv_rank
    page = store.shape[1]
    dp_size = lax.axis_size("dp")
    tp_size = lax.axis_size("tp")
    z = lax.axis_index("tp")
    split = page // tp_size
    cols = kv_rank // LANES

    others = sorted(range(1, tp_size), key=lambda i: -min(i, tp_size - i))
    place = jnp.stack([z] + [z ^ i for i in others]).astype(jnp.int32)
    origins = ((z + jnp.arange(tp_size, dtype=jnp.int32)) % tp_size).astype(jnp.int32)
    own_rows = rows // tp_size
    token = z * own_rows + jnp.arange(own_rows, dtype=jnp.int32)
    position = jnp.where(token // new_len == 0, prefix_len[0], prefix_len[1]) + token % new_len
    piece = lax.dynamic_slice_in_dim(store, z * split, split, axis=1)

    def swap(given, far):
        return lax.ppermute(given, "tp", [(i, i ^ far) for i in range(tp_size)])

    want, pick = plan(page_owner[:, :, 0], page_slot, dp_size)
    asked = lax.all_to_all(want, "dp", split_axis=0, concat_axis=0, tiled=True)

    reply = gather_pages(asked, piece)
    reply, hidden_in, place, position = lax.optimization_barrier(
        (reply, hidden_in, place, position)
    )
    fetched = lax.all_to_all(reply, "dp", split_axis=0, concat_axis=0, tiled=True)

    cosine, sine = turn_tables(position, rope_width // 2)
    gain = latent_gain[None, :]
    part = jnp.dot(hidden_in, kv_down, preferred_element_type=F32)
    kept, *gives = deal(place, part, tp_size)
    got = [swap(given, i) for i, given in zip(others, gives)]
    fresh = finish_latents(kept, gain, cosine, sine, got)
    fetched, fresh, q_nope = lax.optimization_barrier((fetched, fresh, q_nope))

    query = queries(q_nope, q_rope, absorb_k)
    attention = functools.partial(
        attend,
        query,
        origins=origins,
        prefix_len=prefix_len,
        factor=math.log2(math.e) / math.sqrt(nope_width + rope_width),
        page=page,
        split=split,
    )
    up = [(i, (i + 1) % tp_size) for i in range(tp_size)]
    down = [(i, (i - 1) % tp_size) for i in range(tp_size)]
    own = select_pages(pick, fetched.reshape(2 * dp_size, split, lat_width), fresh, cols)
    right, left = lax.ppermute(own, "tp", up), lax.ppermute(own, "tp", down)
    state = attention(blocks=[[own]], steps=(0,))
    right, left, state = lax.optimization_barrier((right, left, state))
    blocks, steps = [[right], [left]], (tp_size - 1, 1)
    seen = [(0, own), (tp_size - 1, right), (1, left)]
    for far in range(2, tp_size // 2):
        next_right = lax.ppermute(right, "tp", up)
        next_left = lax.ppermute(left, "tp", down)
        state = attention(blocks=blocks, steps=steps, state=state)
        right, state = lax.optimization_barrier((next_right, state))
        left = next_left
        blocks, steps = [[right], [left]], (tp_size - far, far)
        seen += [(tp_size - far, right), (far, left)]
    cut = (2 * cols + 1) * 2 // 3 * LANES
    last = [lax.ppermute(right[:cut], "tp", up), lax.ppermute(left[cut:], "tp", down)]
    state = attention(blocks=blocks, steps=steps, state=state)
    attn_out, turned = attention(
        blocks=[last],
        steps=(tp_size // 2,),
        state=state,
        absorb_v=absorb_v,
        seen=tuple(seen),
    )
    return attn_out, turned.T


def solution(mesh):
    placed = (
        P("dp", "tp"),
        P("tp", None),
        P(),
        P("dp", "tp"),
        P("dp", "tp"),
        P("tp", None, None),
        P("tp", None, None),
        P("dp", None, None),
        P("dp", None, None),
        P("dp", None),
        P("dp"),
    )
    return jax.shard_map(
        shards,
        mesh=mesh,
        in_specs=placed,
        out_specs=(P("dp", "tp"), P("dp", None)),
        check_vma=False,
    )
```
